32 devices in a mesh: lat: 4 (over y, x), lon: 8 (over z, core).
Axes of the slice: x: 2, y: 2, z: 4, core: 2. Of those that a mesh axis runs over, the one named last changes fastest.
Arguments:
- field: bfloat16 [48, 384, 360], P('lat', None, 'lon'), may hold values from -6 to 6
- support: int32 [48, 3], P('lat'), may hold values from 0 to 47, as said below
- spec_one: float32 [2, 3, 48, 3, 180], P(None, None, 'lat'), may hold values from -3 to 3
- theta_one: float32 [384, 3], replicated, may hold values from -3 to 3
- spec_two: float32 [2, 3, 48, 3, 180], P(None, None, 'lat'), may hold values from -3 to 3
- theta_two: float32 [384, 3], replicated, may hold values from -3 to 3
- norm_gain: float32 [384], replicated, may hold values from 0.25 to 1.75
- w_in: bfloat16 [1536, 384], P('lon'), may hold values from -0.3125 to 0.3125
- w_out: bfloat16 [1536, 384], P('lon'), may hold values from -0.15625 to 0.15625
Outputs:
- result: bfloat16 [48, 384, 360], P('lat', None, 'lon')
The draws below stay inside these ranges and needn't reach their ends.
Inputs may be any that keep to these rules, and one draw needn't show every extreme that they name: support[i, 0] = i; every other entry lies within 2 rows of i, clipped to the grid.
All inputs are finite; a program needn't handle non-finite values.
Results may differ from the reference program's by a relative error of at most 0.0072.
Values may be sent and summed in bfloat16 or wider, within the bound.
A program may use at most 64 MiB of HBM per device.

```python
import math
import jax
import jax.numpy as jnp
from jax import lax

C = 384
FF = 1536
B = 3
K = 3
HALO = 2
H = 48
L = 360
M = 180


def draw_support(key, part):
    offsets = jax.random.randint(key, (H, K), -HALO, HALO + 1)
    rows = jnp.arange(H, dtype=jnp.int32)[:, None]
    picked = jnp.clip(rows + offsets, 0, H - 1)
    picked = picked.at[:, 0].set(jnp.arange(H, dtype=jnp.int32))
    return picked.astype(jnp.int32)


def level_of(rng, dims, shards, smallest, top_value):
    def one(position, shards_of):
        heights = jax.random.uniform(jax.random.fold_in(jax.random.fold_in(rng, 6), position), (shards_of,), jnp.float32, smallest / len(shards), top_value / len(shards))
        return jnp.repeat(jnp.exp(heights), dims[position] // shards_of).reshape((-1,) + (1,) * (len(dims) - position - 1))

    loudness = one(*shards[0])
    for cut in shards[1:]:
        loudness = loudness * one(*cut)
    return loudness


def gaussian(own_key, shape, deviation, most, shards=(), held_as=jnp.bfloat16):
    level = level_of(own_key, shape, shards, -0.22, 0.18) if shards else 1.0
    array = jax.random.normal(own_key, shape, jnp.float32) * deviation * level
    return jnp.minimum(jnp.maximum(array, -most), most).astype(held_as)


def setup_inputs(seed: int = 0) -> dict:
    splits = jax.random.split(jax.random.key(seed), 10)
    field = gaussian(splits[0], (H, C, L), 1.0, 6.0, ((0, 4), (2, 8)))
    support = draw_support(jax.random.fold_in(splits[9], 71), 0)
    spec_one = gaussian(splits[2], (2, B, H, K, M), 0.5, 3.0, ((2, 4),), jnp.float32)
    theta_one = gaussian(splits[3], (C, B), 0.5, 3.0, (), jnp.float32)
    spec_two = gaussian(splits[4], (2, B, H, K, M), 0.5, 3.0, ((2, 4),), jnp.float32)
    theta_two = gaussian(splits[5], (C, B), 0.5, 3.0, (), jnp.float32)
    norm_gain = jnp.clip(1.0 + 0.15 * jax.random.normal(splits[6], (C,), jnp.float32), 0.25, 1.75)
    w_in = gaussian(splits[7], (FF, C), C ** -0.5, 0.3125, ((0, 8),))
    w_out = gaussian(splits[8], (FF, C), FF ** -0.5, 0.15625, ((0, 8),))
    return dict(field=field, support=support, spec_one=spec_one, theta_one=theta_one, spec_two=spec_two, theta_two=theta_two, norm_gain=norm_gain, w_in=w_in, w_out=w_out)


def build_tables(circle):
    half = circle // 2
    lons = jnp.arange(circle, dtype=jnp.int32)
    modes = jnp.arange(half, dtype=jnp.int32)
    phase = (lons[:, None] * modes[None, :] % circle).astype(jnp.float32) * (2.0 * math.pi / circle)
    forward = jnp.concatenate([jnp.cos(phase), -jnp.sin(phase)], axis=1).astype(jnp.bfloat16)
    weights = jnp.where(modes == 0, 1.0, 2.0).astype(jnp.float32) / circle
    inverse = jnp.concatenate([weights[:, None] * jnp.cos(phase).T, -weights[:, None] * jnp.sin(phase).T], axis=0).astype(jnp.bfloat16)
    return (forward, inverse)

def conv_rows(source, support, spec, theta, forward, inverse):
    spectra = jnp.dot(source.reshape(H * C, L), forward, preferred_element_type=jnp.float32).reshape(H, C, 2 * M)
    spec_re = jnp.transpose(spec[0], (1, 0, 2, 3))
    spec_im = jnp.transpose(spec[1], (1, 0, 2, 3))

    def one_row(items):
        rows_idx, s_re, s_im = items
        picked = spectra[rows_idx]
        g_re = picked[:, :, :M]
        g_im = picked[:, :, M:]
        hp = lax.Precision.HIGHEST
        p_re = jnp.einsum('cb,bkm,kcm->cm', theta, s_re, g_re, precision=hp) - jnp.einsum('cb,bkm,kcm->cm', theta, s_im, g_im, precision=hp)
        p_im = jnp.einsum('cb,bkm,kcm->cm', theta, s_re, g_im, precision=hp) + jnp.einsum('cb,bkm,kcm->cm', theta, s_im, g_re, precision=hp)
        packed = jnp.concatenate([p_re, p_im], axis=1).astype(jnp.bfloat16)
        return jnp.dot(packed, inverse, preferred_element_type=jnp.float32).astype(jnp.bfloat16)
    return lax.map(one_row, (support, spec_re, spec_im))

def reference(field, support, spec_one, theta_one, spec_two, theta_two, norm_gain, w_in, w_out):
    forward, inverse = build_tables(L)
    first = conv_rows(field, support, spec_one, theta_one, forward, inverse)
    values = first.astype(jnp.float32)
    mean = lax.optimization_barrier(jnp.mean(values, axis=1, keepdims=True))
    meansq = lax.optimization_barrier(jnp.mean(values * values, axis=1, keepdims=True))
    normed = ((values - mean) * lax.rsqrt(meansq - mean * mean + 1e-05) * norm_gain[None, :, None]).astype(jnp.bfloat16)
    second = conv_rows(normed, support, spec_two, theta_two, forward, inverse)
    w_in32 = w_in.astype(jnp.float32)
    w_out32 = w_out.astype(jnp.float32)

    def mlp_row(items):
        row_in, row_field = items
        hidden = jax.nn.gelu(jnp.einsum('cl,fc->fl', row_in.astype(jnp.float32), w_in32)).astype(jnp.bfloat16)
        update = jnp.einsum('fl,fc->cl', hidden.astype(jnp.float32), w_out32)
        return (row_field.astype(jnp.float32) + update).astype(jnp.bfloat16)
    return lax.map(mlp_row, (second, field))
```

```python
import functools
import math

import jax
import jax.numpy as jnp
import numpy as np
from jax import lax
from jax.experimental import pallas as pl
from jax.experimental.pallas import tpu as pltpu
from jax.sharding import PartitionSpec as P

HALO = 2
MESH = pl.DeviceIdType.MESH
F32 = jnp.float32
BF16 = jnp.bfloat16


def round_up(value, step):
    return -(-value // step) * step


def tables(circle, n, lons, lon_pad, mode_pad):
    half = circle // 2
    grid = np.arange(circle)[:, None] * np.arange(half)[None, :] % circle
    phase = grid.astype(np.float64) * (2.0 * math.pi / circle)
    cos, sin = np.cos(phase), np.sin(phase)
    weights = np.where(np.arange(half) == 0, 1.0, 2.0) / circle
    forward = np.zeros((n, lon_pad, 2, mode_pad), np.float32)
    forward[:, :lons, 0, :half] = cos.reshape(n, lons, half)
    forward[:, :lons, 1, :half] = -sin.reshape(n, lons, half)
    inverse_t = np.zeros((n, lon_pad, 2, mode_pad), np.float32)
    inverse_t[:, :lons, 0, :half] = (cos * weights).reshape(n, lons, half)
    inverse_t[:, :lons, 1, :half] = (-sin * weights).reshape(n, lons, half)
    forward = forward.reshape(n * lon_pad, 2 * mode_pad)
    inverse_t = inverse_t.reshape(n * lon_pad, 2 * mode_pad)
    eye = np.eye(lon_pad, lons, dtype=np.float32)
    return [jnp.asarray(t, BF16) for t in (eye, forward, inverse_t.T, inverse_t)]


def conv_kernel(
    n, n_lat, chans, half,
    support, field, eye, forward, inverse, inverse_t, spec_one, theta_one, spec_two, theta_two, gain,
    out,
    send_t, circ_t, ext_one, ext_two, spectra, packed, first, part, sums, totals, second_t,
    a_send, a_recv, b_send, b_recv, c_send, c_recv, d_send, d_recv, h_send, h_recv,
):
    rows = field.shape[0]
    cp = field.shape[1] // n
    lon_pad = eye.shape[0]
    mode_pad = forward.shape[1] // 2
    me = lax.axis_index("lon")
    lat = lax.axis_index("lat")
    up = lax.rem(lat + 1, n_lat)
    down = lax.rem(lat + n_lat - 1, n_lat)
    per = part.shape[1]

    def peer(o):
        return lax.rem(me + o, n)

    barrier = pltpu.get_barrier_semaphore()
    for o in range(1, n):
        pl.semaphore_signal(barrier, inc=1, device_id=(lat, peer(o)), device_id_type=MESH)
    for side in (up, down):
        pl.semaphore_signal(barrier, inc=1, device_id=(side, me), device_id_type=MESH)

    def block_of(d):
        x = field[:, pl.ds(pl.multiple_of(d * cp, 16), cp), :].reshape(rows * cp, field.shape[2])
        turned = lax.dot_general(eye[...], x, (((1,), (1,)), ((), ())), preferred_element_type=F32)
        return turned.astype(BF16)

    def exchange(srcs, dst, send, recv):
        copies = []
        for o in range(1, n):
            copies.append(pltpu.make_async_remote_copy(
                src_ref=srcs(o), dst_ref=dst, send_sem=send.at[o], recv_sem=recv.at[o],
                device_id=(lat, peer(o)), device_id_type=MESH))
        return copies

    mine = pl.multiple_of(me * lon_pad, 16)
    copies_a = exchange(lambda o: send_t.at[o], circ_t.at[pl.ds(mine, lon_pad)], a_send, a_recv)
    for o in range(1, n):
        send_t[o] = block_of(peer(o))
        if o == 1:
            pl.semaphore_wait(barrier, n + 1)
        copies_a[o - 1].start()
    circ_t[pl.ds(mine, lon_pad)] = block_of(me)
    packed[...] = jnp.zeros_like(packed)
    part[...] = jnp.zeros_like(part)

    own = slice(HALO * cp, (HALO + rows) * cp)

    def halo(ext, which):
        width = HALO * cp
        low = pltpu.make_async_remote_copy(
            src_ref=ext.at[pl.ds(width, width)], dst_ref=ext.at[pl.ds(width + rows * cp, width)],
            send_sem=h_send.at[which, 0], recv_sem=h_recv.at[which, 0],
            device_id=(down, me), device_id_type=MESH)
        high = pltpu.make_async_remote_copy(
            src_ref=ext.at[pl.ds(rows * cp, width)], dst_ref=ext.at[pl.ds(0, width)],
            send_sem=h_send.at[which, 1], recv_sem=h_recv.at[which, 1],
            device_id=(up, me), device_id_type=MESH)
        return low, high

    def mix(ext, halos, spec, theta):
        def dft(start, count):
            x = ext[start * cp:(start + count) * cp, :]
            spectra[start:start + count] = jnp.dot(
                x, forward[...], preferred_element_type=F32).reshape(count, cp, 2 * mode_pad)

        dft(HALO, rows)
        for copy in halos:
            copy.wait_recv()
        dft(0, HALO)
        dft(HALO + rows, HALO)
        th = theta[pl.ds(pl.multiple_of(me * cp, 8), cp), :]
        cols = [th[:, b:b + 1] for b in range(th.shape[1])]

        def row(i, carry):
            p_re = jnp.zeros((cp, half), F32)
            p_im = jnp.zeros((cp, half), F32)
            for k in range(support.shape[1]):
                r = jnp.clip(support[i, k] - lat * rows + HALO, 0, rows + 2 * HALO - 1)
                g = spectra[r]
                g_re, g_im = g[:, :half], g[:, mode_pad:mode_pad + half]
                w_re = sum(cols[b] * spec[0, b, i][k:k + 1, :] for b in range(len(cols)))
                w_im = sum(cols[b] * spec[1, b, i][k:k + 1, :] for b in range(len(cols)))
                p_re += w_re * g_re - w_im * g_im
                p_im += w_re * g_im + w_im * g_re
            packed[i, :, :half] = p_re.astype(BF16)
            packed[i, :, mode_pad:mode_pad + half] = p_im.astype(BF16)
            return carry

        lax.fori_loop(0, rows, row, 0)
        return packed[...].reshape(rows * cp, 2 * mode_pad)

    for copy in copies_a:
        copy.wait_recv()
    ext_one[own, :] = circ_t[...].T
    halo_one = halo(ext_one, 0)
    for copy in halo_one:
        copy.start()
    spectrum = mix(ext_one, halo_one, spec_one, theta_one)
    values = jnp.dot(spectrum, inverse[...], preferred_element_type=F32).astype(BF16)
    first[...] = values.reshape(first.shape)

    for i in range(rows):
        v = first[i].astype(F32)
        part[i // per, i % per] = jnp.sum(v, axis=0)
        j = rows + i
        part[j // per, j % per] = jnp.sum(v * v, axis=0)
    copies_b = exchange(lambda o: part.at[peer(o)], sums.at[me], b_send, b_recv)
    for copy in copies_b:
        copy.start()
    sums[me] = part[me]
    for copy in copies_b:
        copy.wait_recv()
    totals[me] = jnp.sum(sums[...], axis=0)
    copies_c = exchange(lambda o: totals.at[me], totals.at[me], c_send, c_recv)
    for copy in copies_c:
        copy.start()
    for copy in copies_c:
        copy.wait_recv()
    scale = gain[pl.ds(pl.multiple_of(me * cp, 8), cp), :]
    halo_two = halo(ext_two, 1)

    def normalise(i):
        j = rows + i
        mean = totals[i // per, i % per][None, :] * (1.0 / chans)
        meansq = totals[j // per, j % per][None, :] * (1.0 / chans)
        v = first[i].astype(F32)
        v = (v - mean) * lax.rsqrt(meansq - mean * mean + 1e-05) * scale
        ext_two[(HALO + i) * cp:(HALO + i + 1) * cp, :] = v.astype(BF16)

    edges = list(range(HALO)) + list(range(rows - HALO, rows))
    for i in edges:
        normalise(i)
    for copy in halo_two:
        copy.start()
    for i in range(HALO, rows - HALO):
        normalise(i)
    spectrum = mix(ext_two, halo_two, spec_two, theta_two)
    second_t[...] = lax.dot_general(
        inverse_t[...], spectrum, (((1,), (1,)), ((), ())), preferred_element_type=F32
    ).astype(BF16).reshape(second_t.shape)
    copies_d = exchange(lambda o: second_t.at[peer(o)], out.at[me], d_send, d_recv)
    for copy in copies_d:
        copy.start()
    out[me] = second_t[me]
    for copy in copies_d:
        copy.wait_recv()
    for copy in copies_a + copies_b + copies_c + copies_d:
        copy.wait_send()
    for copy in halo_one + halo_two:
        copy.wait_send()


def shards(n, n_lat, field, support, spec_one, theta_one, spec_two, theta_two, norm_gain, w_in, w_out):
    rows, chans, lons = field.shape
    circle = lons * n
    half = circle // 2
    part = chans // n
    cp = round_up(part, 16)
    lon_pad = round_up(lons, 16)
    mode_pad = round_up(half, 128)
    eye, forward, inverse, inverse_t = tables(circle, n, lons, lon_pad, mode_pad)

    def spread(x, axis):
        if cp == part:
            return x
        shape = x.shape
        x = x.reshape(shape[:axis] + (n, part) + shape[axis + 1:])
        pads = [(0, 0)] * x.ndim
        pads[axis + 1] = (0, cp - part)
        return jnp.pad(x, pads).reshape(shape[:axis] + (n * cp,) + shape[axis + 1:])

    per = -(-2 * rows // n)
    lanes = n * lon_pad
    vmem = pl.BlockSpec(memory_space=pltpu.VMEM)
    smem = pl.BlockSpec(memory_space=pltpu.SMEM)
    pair = pltpu.SemaphoreType.DMA((n,))
    out = pl.pallas_call(
        functools.partial(conv_kernel, n, n_lat, chans, half),
        out_shape=jax.ShapeDtypeStruct((n, lon_pad, rows * cp), BF16),
        in_specs=[smem] + [vmem] * 10,
        out_specs=vmem,
        scratch_shapes=[
            pltpu.VMEM((n, lon_pad, rows * cp), BF16),
            pltpu.VMEM((lanes, rows * cp), BF16),
            pltpu.VMEM(((rows + 2 * HALO) * cp, lanes), BF16),
            pltpu.VMEM(((rows + 2 * HALO) * cp, lanes), BF16),
            pltpu.VMEM((rows + 2 * HALO, cp, 2 * mode_pad), F32),
            pltpu.VMEM((rows, cp, 2 * mode_pad), BF16),
            pltpu.VMEM((rows, cp, lanes), BF16),
            pltpu.VMEM((n, per, lanes), F32),
            pltpu.VMEM((n, per, lanes), F32),
            pltpu.VMEM((n, per, lanes), F32),
            pltpu.VMEM((n, lon_pad, rows * cp), BF16),
        ] + [pair] * 8 + [pltpu.SemaphoreType.DMA((2, 2))] * 2,
        compiler_params=pltpu.CompilerParams(
            collective_id=0, has_side_effects=True, vmem_limit_bytes=50 * 2**20),
        name="convs",
    )(
        support, spread(field, 1), eye, forward, inverse, inverse_t,
        spec_one, spread(theta_one, 0), spec_two, spread(theta_two, 0), spread(norm_gain, 0)[:, None],
    )
    piece_in = lax.all_gather(w_in, "lon", axis=0, tiled=True)
    piece_out = lax.all_gather(w_out, "lon", axis=0, tiled=True)
    cells = out.reshape(n, lon_pad, rows, cp)[:, :lons, :, :part]
    cells = cells.transpose(2, 0, 3, 1).reshape(rows, chans, lons)
    hidden = jax.nn.gelu(
        jnp.einsum("hcl,fc->hfl", cells, piece_in, preferred_element_type=F32)
    ).astype(BF16)
    update = jnp.einsum("hfl,fc->hcl", hidden, piece_out, preferred_element_type=F32)
    return (field.astype(F32) + update).astype(BF16)


def solution(mesh):
    in_specs = (
        P("lat", None, "lon"),
        P("lat", None),
        P(None, None, "lat", None, None),
        P(),
        P(None, None, "lat", None, None),
        P(),
        P(),
        P("lon", None),
        P("lon", None),
    )
    body = functools.partial(shards, mesh.shape["lon"], mesh.shape["lat"])
    return jax.shard_map(
        body, mesh=mesh, in_specs=in_specs, out_specs=P("lat", None, "lon"), check_vma=False)
```

```python
import functools
import math

import jax
import jax.numpy as jnp
import numpy as np
from jax import lax
from jax.experimental import pallas as pl
from jax.experimental.pallas import tpu as pltpu
from jax.sharding import PartitionSpec as P

HALO = 2
CORES = 2
MESH = pl.DeviceIdType.MESH
F32 = jnp.float32
BF16 = jnp.bfloat16


def round_up(value, step):
    return -(-value // step) * step


def tables(circle, n, lons, lon_pad, mode_pad):
    half = circle // 2
    grid = np.arange(circle)[:, None] * np.arange(half)[None, :] % circle
    phase = grid.astype(np.float64) * (2.0 * math.pi / circle)
    cos, sin = np.cos(phase), np.sin(phase)
    weights = np.where(np.arange(half) == 0, 1.0, 2.0) / circle
    forward = np.zeros((n, lon_pad, 2, mode_pad), np.float32)
    forward[:, :lons, 0, :half] = cos.reshape(n, lons, half)
    forward[:, :lons, 1, :half] = -sin.reshape(n, lons, half)
    inverse_t = np.zeros((n, lon_pad, 2, mode_pad), np.float32)
    inverse_t[:, :lons, 0, :half] = (cos * weights).reshape(n, lons, half)
    inverse_t[:, :lons, 1, :half] = (-sin * weights).reshape(n, lons, half)
    forward = forward.reshape(n * lon_pad, 2 * mode_pad)
    inverse_t = inverse_t.reshape(n * lon_pad, 2 * mode_pad)
    eye = np.eye(lon_pad, lons, dtype=np.float32)
    return [jnp.asarray(t, BF16) for t in (eye, forward, inverse_t.T, inverse_t)]


def conv_kernel(
    n, n_lat, chans, half, gather,
    support, field, eye, forward, inverse, inverse_t, spec_one, theta_one, spec_two, theta_two, gain, w_in, w_out,
    out, all_in, all_out,
    send_t, circ_t, ext_one, ext_two, spectra, packed, first, part, sums, totals, second_t,
    a_send, a_recv, b_send, b_recv, c_send, c_recv, d_send, d_recv, h_send, h_recv,
    u_send, u_recv, v_send, v_recv, w_send, w_recv,
):
    rows = field.shape[0]
    cp = field.shape[1] // n
    lon_pad = eye.shape[0]
    mode_pad = forward.shape[1] // 2
    me = lax.axis_index("lon")
    lat = lax.axis_index("lat")
    up = lax.rem(lat + 1, n_lat)
    down = lax.rem(lat + n_lat - 1, n_lat)
    per = part.shape[1]

    def peer(o):
        return lax.rem(me + o, n)

    barrier = pltpu.get_barrier_semaphore()
    for o in range(1, n):
        pl.semaphore_signal(barrier, inc=1, device_id=(lat, peer(o)), device_id_type=MESH)
    for o in range(1, n_lat):
        pl.semaphore_signal(
            barrier, inc=1, device_id=(lax.rem(lat + o, n_lat), me), device_id_type=MESH)

    def block_of(d):
        x = field[:, pl.ds(pl.multiple_of(d * cp, 16), cp), :].reshape(rows * cp, field.shape[2])
        turned = lax.dot_general(eye[...], x, (((1,), (1,)), ((), ())), preferred_element_type=F32)
        return turned.astype(BF16)

    def exchange(srcs, dst, send, recv):
        copies = []
        for o in range(1, n):
            copies.append(pltpu.make_async_remote_copy(
                src_ref=srcs(o), dst_ref=dst, send_sem=send.at[o], recv_sem=recv.at[o],
                device_id=(lat, peer(o)), device_id_type=MESH))
        return copies

    mine = pl.multiple_of(me * lon_pad, 16)
    copies_a = exchange(lambda o: send_t.at[o], circ_t.at[pl.ds(mine, lon_pad)], a_send, a_recv)
    for o in range(1, n):
        send_t[o] = block_of(peer(o))
        if o == 1:
            pl.semaphore_wait(barrier, n + n_lat - 2)
        copies_a[o - 1].start()
    circ_t[pl.ds(mine, lon_pad)] = block_of(me)
    packed[...] = jnp.zeros_like(packed)
    part[...] = jnp.zeros_like(part)

    pairs = ((w_in, all_in), (w_out, all_out)) if gather else ()
    core = lax.rem(me, CORES)
    chip = me // CORES

    def remote(src, dst, send, recv, device):
        return pltpu.make_async_remote_copy(
            src_ref=src, dst_ref=dst, send_sem=send, recv_sem=recv,
            device_id=device, device_id_type=MESH)

    copies_u, copies_v, copies_w = [], [], []
    for m, (shard, whole) in enumerate(pairs):
        piece = whole.shape[3]
        share = pl.ds(pl.multiple_of(lat * piece, 16), piece)
        for o in range(1, n // CORES):
            copies_u.append(remote(
                shard.at[share], whole.at[core, lat, chip], u_send.at[m, o], u_recv.at[m, o],
                (lat, peer(CORES * o))))
        for o in range(1, n_lat):
            copies_v.append(remote(
                whole.at[core, lat], whole.at[core, lat], v_send.at[m, o], v_recv.at[m, o],
                (lax.rem(lat + o, n_lat), me)))
        copies_w.append(remote(
            whole.at[core], whole.at[core], w_send.at[m], w_recv.at[m],
            (lat, me + 1 - 2 * core)))
        whole[core, lat, chip] = shard[share, :]

    own = slice(HALO * cp, (HALO + rows) * cp)

    def halo(ext, which):
        width = HALO * cp
        low = pltpu.make_async_remote_copy(
            src_ref=ext.at[pl.ds(width, width)], dst_ref=ext.at[pl.ds(width + rows * cp, width)],
            send_sem=h_send.at[which, 0], recv_sem=h_recv.at[which, 0],
            device_id=(down, me), device_id_type=MESH)
        high = pltpu.make_async_remote_copy(
            src_ref=ext.at[pl.ds(rows * cp, width)], dst_ref=ext.at[pl.ds(0, width)],
            send_sem=h_send.at[which, 1], recv_sem=h_recv.at[which, 1],
            device_id=(up, me), device_id_type=MESH)
        return low, high

    def mix(ext, halos, spec, theta):
        def dft(start, count):
            x = ext[start * cp:(start + count) * cp, :]
            spectra[start:start + count] = jnp.dot(
                x, forward[...], preferred_element_type=F32).reshape(count, cp, 2 * mode_pad)

        dft(HALO, rows)
        for copy in halos:
            copy.wait_recv()
        dft(0, HALO)
        dft(HALO + rows, HALO)
        th = theta[pl.ds(pl.multiple_of(me * cp, 8), cp), :]
        cols = [th[:, b:b + 1] for b in range(th.shape[1])]

        def row(i, carry):
            p_re = jnp.zeros((cp, half), F32)
            p_im = jnp.zeros((cp, half), F32)
            for k in range(support.shape[1]):
                r = jnp.clip(support[i, k] - lat * rows + HALO, 0, rows + 2 * HALO - 1)
                g = spectra[r]
                g_re, g_im = g[:, :half], g[:, mode_pad:mode_pad + half]
                w_re = sum(cols[b] * spec[0, b, i][k:k + 1, :] for b in range(len(cols)))
                w_im = sum(cols[b] * spec[1, b, i][k:k + 1, :] for b in range(len(cols)))
                p_re += w_re * g_re - w_im * g_im
                p_im += w_re * g_im + w_im * g_re
            packed[i, :, :half] = p_re.astype(BF16)
            packed[i, :, mode_pad:mode_pad + half] = p_im.astype(BF16)
            return carry

        lax.fori_loop(0, rows, row, 0)
        return packed[...].reshape(rows * cp, 2 * mode_pad)

    for copy in copies_a:
        copy.wait_recv()
    ext_one[own, :] = circ_t[...].T
    halo_one = halo(ext_one, 0)
    for copy in halo_one:
        copy.start()
    for copy in copies_u:
        copy.start()
    spectrum = mix(ext_one, halo_one, spec_one, theta_one)
    values = jnp.dot(spectrum, inverse[...], preferred_element_type=F32).astype(BF16)
    first[...] = values.reshape(first.shape)

    for i in range(rows):
        v = first[i].astype(F32)
        part[i // per, i % per] = jnp.sum(v, axis=0)
        j = rows + i
        part[j // per, j % per] = jnp.sum(v * v, axis=0)
    copies_b = exchange(lambda o: part.at[peer(o)], sums.at[me], b_send, b_recv)
    for copy in copies_b:
        copy.start()
    sums[me] = part[me]
    for copy in copies_u:
        copy.wait_recv()
    for copy in copies_v:
        copy.start()
    for copy in copies_b:
        copy.wait_recv()
    totals[me] = jnp.sum(sums[...], axis=0)
    copies_c = exchange(lambda o: totals.at[me], totals.at[me], c_send, c_recv)
    for copy in copies_c:
        copy.start()
    for copy in copies_c:
        copy.wait_recv()
    scale = gain[pl.ds(pl.multiple_of(me * cp, 8), cp), :]
    halo_two = halo(ext_two, 1)

    def normalise(i):
        j = rows + i
        mean = totals[i // per, i % per][None, :] * (1.0 / chans)
        meansq = totals[j // per, j % per][None, :] * (1.0 / chans)
        v = first[i].astype(F32)
        v = (v - mean) * lax.rsqrt(meansq - mean * mean + 1e-05) * scale
        ext_two[(HALO + i) * cp:(HALO + i + 1) * cp, :] = v.astype(BF16)

    edges = list(range(HALO)) + list(range(rows - HALO, rows))
    for i in edges:
        normalise(i)
    for copy in halo_two:
        copy.start()
    for i in range(HALO, rows - HALO):
        normalise(i)
    spectrum = mix(ext_two, halo_two, spec_two, theta_two)
    second_t[...] = lax.dot_general(
        inverse_t[...], spectrum, (((1,), (1,)), ((), ())), preferred_element_type=F32
    ).astype(BF16).reshape(second_t.shape)
    copies_d = exchange(lambda o: second_t.at[peer(o)], out.at[me], d_send, d_recv)
    for copy in copies_d:
        copy.start()
    for copy in copies_v:
        copy.wait_recv()
    for copy in copies_w:
        copy.start()
    out[me] = second_t[me]
    for copy in copies_d + copies_w:
        copy.wait_recv()
    for copy in copies_a + copies_b + copies_c + copies_d + copies_u + copies_v + copies_w:
        copy.wait_send()
    for copy in halo_one + halo_two:
        copy.wait_send()


def shards(n, n_lat, field, support, spec_one, theta_one, spec_two, theta_two, norm_gain, w_in, w_out):
    rows, chans, lons = field.shape
    circle = lons * n
    half = circle // 2
    part = chans // n
    cp = round_up(part, 16)
    lon_pad = round_up(lons, 16)
    mode_pad = round_up(half, 128)
    eye, forward, inverse, inverse_t = tables(circle, n, lons, lon_pad, mode_pad)

    def spread(x, axis):
        if cp == part:
            return x
        shape = x.shape
        x = x.reshape(shape[:axis] + (n, part) + shape[axis + 1:])
        pads = [(0, 0)] * x.ndim
        pads[axis + 1] = (0, cp - part)
        return jnp.pad(x, pads).reshape(shape[:axis] + (n * cp,) + shape[axis + 1:])

    per = -(-2 * rows // n)
    lanes = n * lon_pad
    vmem = pl.BlockSpec(memory_space=pltpu.VMEM)
    smem = pl.BlockSpec(memory_space=pltpu.SMEM)
    pair = pltpu.SemaphoreType.DMA((n,))
    piece = w_in.shape[0] // n_lat
    gather = n % CORES == 0 and w_in.shape[0] % n_lat == 0 and piece % 16 == 0
    if not gather:
        piece = 16
    weights = jax.ShapeDtypeStruct((CORES, n_lat, n // CORES, piece, chans), BF16)
    out, piece_in, piece_out = pl.pallas_call(
        functools.partial(conv_kernel, n, n_lat, chans, half, gather),
        out_shape=(jax.ShapeDtypeStruct((n, lon_pad, rows * cp), BF16), weights, weights),
        in_specs=[smem] + [vmem] * 12,
        out_specs=(vmem, vmem, vmem),
        scratch_shapes=[
            pltpu.VMEM((n, lon_pad, rows * cp), BF16),
            pltpu.VMEM((lanes, rows * cp), BF16),
            pltpu.VMEM(((rows + 2 * HALO) * cp, lanes), BF16),
            pltpu.VMEM(((rows + 2 * HALO) * cp, lanes), BF16),
            pltpu.VMEM((rows + 2 * HALO, cp, 2 * mode_pad), F32),
            pltpu.VMEM((rows, cp, 2 * mode_pad), BF16),
            pltpu.VMEM((rows, cp, lanes), BF16),
            pltpu.VMEM((n, per, lanes), F32),
            pltpu.VMEM((n, per, lanes), F32),
            pltpu.VMEM((n, per, lanes), F32),
            pltpu.VMEM((n, lon_pad, rows * cp), BF16),
        ] + [pair] * 8 + [pltpu.SemaphoreType.DMA((2, 2))] * 2
        + [pltpu.SemaphoreType.DMA((2, max(1, n // CORES)))] * 2
        + [pltpu.SemaphoreType.DMA((2, n_lat))] * 2
        + [pltpu.SemaphoreType.DMA((2,))] * 2,
        compiler_params=pltpu.CompilerParams(
            collective_id=0, has_side_effects=True, vmem_limit_bytes=50 * 2**20),
        name="convs",
    )(
        support, spread(field, 1), eye, forward, inverse, inverse_t,
        spec_one, spread(theta_one, 0), spec_two, spread(theta_two, 0), spread(norm_gain, 0)[:, None], w_in, w_out,
    )
    if gather:
        piece_in, piece_out = piece_in.reshape(-1, chans), piece_out.reshape(-1, chans)
    else:
        piece_in = lax.all_gather(w_in, "lon", axis=0, tiled=True)
        piece_out = lax.all_gather(w_out, "lon", axis=0, tiled=True)
    cells = out.reshape(n, lon_pad, rows, cp)[:, :lons, :, :part]
    cells = cells.transpose(2, 0, 3, 1).reshape(rows, chans, lons)
    hidden = jax.nn.gelu(
        jnp.einsum("hcl,fc->hfl", cells, piece_in, preferred_element_type=F32)
    ).astype(BF16)
    update = jnp.einsum("hfl,fc->hcl", hidden, piece_out, preferred_element_type=F32)
    return (field.astype(F32) + update).astype(BF16)


def solution(mesh):
    in_specs = (
        P("lat", None, "lon"),
        P("lat", None),
        P(None, None, "lat", None, None),
        P(),
        P(None, None, "lat", None, None),
        P(),
        P(),
        P("lon", None),
        P("lon", None),
    )
    body = functools.partial(shards, mesh.shape["lon"], mesh.shape["lat"])
    return jax.shard_map(
        body, mesh=mesh, in_specs=in_specs, out_specs=P("lat", None, "lon"), check_vma=False)
```

```python
import functools
import math

import jax
import jax.numpy as jnp
import numpy as np
from jax import lax
from jax.experimental import pallas as pl
from jax.experimental.pallas import tpu as pltpu
from jax.sharding import PartitionSpec as P

HALO = 2
CORES = 2
MESH = pl.DeviceIdType.MESH
F32 = jnp.float32
BF16 = jnp.bfloat16


def round_up(value, step):
    return -(-value // step) * step


def tables(circle, n, lons, lon_pad, mode_pad):
    half = circle // 2
    grid = np.arange(circle)[:, None] * np.arange(half)[None, :] % circle
    phase = grid.astype(np.float64) * (2.0 * math.pi / circle)
    cos, sin = np.cos(phase), np.sin(phase)
    weights = np.where(np.arange(half) == 0, 1.0, 2.0) / circle
    forward = np.zeros((n, lon_pad, 2, mode_pad), np.float32)
    forward[:, :lons, 0, :half] = cos.reshape(n, lons, half)
    forward[:, :lons, 1, :half] = -sin.reshape(n, lons, half)
    inverse_t = np.zeros((n, lon_pad, 2, mode_pad), np.float32)
    inverse_t[:, :lons, 0, :half] = (cos * weights).reshape(n, lons, half)
    inverse_t[:, :lons, 1, :half] = (-sin * weights).reshape(n, lons, half)
    forward = forward.reshape(n * lon_pad, 2 * mode_pad)
    inverse_t = inverse_t.reshape(n * lon_pad, 2 * mode_pad)
    return [jnp.asarray(t, BF16) for t in (forward, inverse_t.T, inverse_t)]


def conv_kernel(
    n, n_lat, chans, half, gather,
    support, field, forward, inverse, inverse_t, spec_one, theta_one, spec_two, theta_two, gain, w_in, w_out,
    out, all_in, all_out,
    send_t, circ_t, ext_one, ext_two, spectra, packed, first, part, sums, totals, second_t,
    columns,
    a_send, a_recv, b_send, b_recv, c_send, c_recv, d_send, d_recv, h_send, h_recv,
    u_send, u_recv, v_send, v_recv, w_send, w_recv,
):
    rows = field.shape[0]
    lons = field.shape[1]
    cp = field.shape[2] // n
    lon_pad = send_t.shape[1]
    mode_pad = forward.shape[1] // 2
    me = lax.axis_index("lon")
    lat = lax.axis_index("lat")
    up = lax.rem(lat + 1, n_lat)
    down = lax.rem(lat + n_lat - 1, n_lat)
    per = part.shape[1]

    def peer(o):
        return lax.rem(me + o, n)

    barrier = pltpu.get_barrier_semaphore()
    for o in range(1, n):
        pl.semaphore_signal(barrier, inc=1, device_id=(lat, peer(o)), device_id_type=MESH)
    for o in range(1, n_lat):
        pl.semaphore_signal(
            barrier, inc=1, device_id=(lax.rem(lat + o, n_lat), me), device_id_type=MESH)

    def exchange(srcs, dst, send, recv):
        copies = []
        for o in range(1, n):
            copies.append(pltpu.make_async_remote_copy(
                src_ref=srcs(o), dst_ref=dst, send_sem=send.at[o], recv_sem=recv.at[o],
                device_id=(lat, peer(o)), device_id_type=MESH))
        return copies

    mine = pl.multiple_of(me * lon_pad, 16)
    copies_a = exchange(lambda o: send_t.at[peer(o)], circ_t.at[pl.ds(mine, lon_pad)], a_send, a_recv)
    send_t[...] = jnp.zeros_like(send_t)
    for i in range(rows):
        x = field[i]
        for d in range(n):
            send_t[d, :lons, i * cp:(i + 1) * cp] = x[:, d * cp:(d + 1) * cp]
    pl.semaphore_wait(barrier, n + n_lat - 2)
    for copy in copies_a:
        copy.start()
    circ_t[pl.ds(mine, lon_pad)] = send_t[me]
    basis = theta_one.shape[0]
    stack = [theta_one[...], theta_two[...], gain[...]]
    stack.append(jnp.zeros((round_up(2 * basis + 1, 8) - 2 * basis - 1, n * cp), F32))
    columns[...] = jnp.concatenate(stack, axis=0).T
    packed[...] = jnp.zeros_like(packed)
    part[...] = jnp.zeros_like(part)

    pairs = ((w_in, all_in), (w_out, all_out)) if gather else ()
    core = lax.rem(me, CORES)
    chip = me // CORES

    def remote(src, dst, send, recv, device):
        return pltpu.make_async_remote_copy(
            src_ref=src, dst_ref=dst, send_sem=send, recv_sem=recv,
            device_id=device, device_id_type=MESH)

    copies_u, copies_v, copies_w = [], [], []
    for m, (shard, whole) in enumerate(pairs):
        piece = whole.shape[3]
        share = pl.ds(pl.multiple_of(lat * piece, 16), piece)
        for o in range(1, n // CORES):
            copies_u.append(remote(
                shard.at[share], whole.at[core, lat, chip], u_send.at[m, o], u_recv.at[m, o],
                (lat, peer(CORES * o))))
        for o in range(1, n_lat):
            copies_v.append(remote(
                whole.at[core, lat], whole.at[core, lat], v_send.at[m, o], v_recv.at[m, o],
                (lax.rem(lat + o, n_lat), me)))
        copies_w.append(remote(
            whole.at[core], whole.at[core], w_send.at[m], w_recv.at[m],
            (lat, me + 1 - 2 * core)))
        whole[core, lat, chip] = shard[share, :]

    own = slice(HALO * cp, (HALO + rows) * cp)

    def halo(ext, which):
        width = HALO * cp
        low = pltpu.make_async_remote_copy(
            src_ref=ext.at[pl.ds(width, width)], dst_ref=ext.at[pl.ds(width + rows * cp, width)],
            send_sem=h_send.at[which, 0], recv_sem=h_recv.at[which, 0],
            device_id=(down, me), device_id_type=MESH)
        high = pltpu.make_async_remote_copy(
            src_ref=ext.at[pl.ds(rows * cp, width)], dst_ref=ext.at[pl.ds(0, width)],
            send_sem=h_send.at[which, 1], recv_sem=h_recv.at[which, 1],
            device_id=(up, me), device_id_type=MESH)
        return low, high

    def mix(ext, halos, spec, theta):
        def dft(start, count):
            x = ext[start * cp:(start + count) * cp, :]
            spectra[start:start + count] = jnp.dot(
                x, forward[...], preferred_element_type=F32).reshape(count, cp, 2 * mode_pad)

        dft(HALO, rows)
        th = columns[pl.ds(pl.multiple_of(me * cp, 8), cp), :]
        cols = [th[:, theta + b:theta + b + 1] for b in range(basis)]

        def row(i, carry):
            p_re = jnp.zeros((cp, half), F32)
            p_im = jnp.zeros((cp, half), F32)
            for k in range(support.shape[0]):
                r = jnp.clip(support[k, i] - lat * rows + HALO, 0, rows + 2 * HALO - 1)
                g = spectra[r]
                g_re, g_im = g[:, :half], g[:, mode_pad:mode_pad + half]
                w_re = sum(cols[b] * spec[b, i, k][0:1, :] for b in range(len(cols)))
                w_im = sum(cols[b] * spec[b, i, k][1:2, :] for b in range(len(cols)))
                p_re += w_re * g_re - w_im * g_im
                p_im += w_re * g_im + w_im * g_re
            packed[i, :, :half] = p_re.astype(BF16)
            packed[i, :, mode_pad:mode_pad + half] = p_im.astype(BF16)
            return carry

        inner = (HALO, rows - HALO) if rows > 2 * HALO else (0, 0)
        lax.fori_loop(inner[0], inner[1], row, 0)
        for copy in halos:
            copy.wait_recv()
        dft(0, HALO)
        dft(HALO + rows, HALO)
        if inner[1]:
            lax.fori_loop(0, HALO, row, 0)
            lax.fori_loop(rows - HALO, rows, row, 0)
        else:
            lax.fori_loop(0, rows, row, 0)
        return packed[...].reshape(rows * cp, 2 * mode_pad)

    for copy in copies_a:
        copy.wait_recv()
    ext_one[own, :] = circ_t[...].T
    halo_one = halo(ext_one, 0)
    for copy in halo_one:
        copy.start()
    for copy in copies_u:
        copy.start()
    spectrum = mix(ext_one, halo_one, spec_one, 0)
    values = jnp.dot(spectrum, inverse[...], preferred_element_type=F32).astype(BF16)
    first[...] = values.reshape(first.shape)

    for i in range(rows):
        v = first[i].astype(F32)
        part[i // per, i % per] = jnp.sum(v, axis=0)
        j = rows + i
        part[j // per, j % per] = jnp.sum(v * v, axis=0)
    copies_b = exchange(lambda o: part.at[peer(o)], sums.at[me], b_send, b_recv)
    for copy in copies_b:
        copy.start()
    sums[me] = part[me]
    for copy in copies_u:
        copy.wait_recv()
    for copy in copies_v:
        copy.start()
    for copy in copies_b:
        copy.wait_recv()
    totals[me] = jnp.sum(sums[...], axis=0)
    copies_c = exchange(lambda o: totals.at[me], totals.at[me], c_send, c_recv)
    for copy in copies_c:
        copy.start()
    for copy in copies_c:
        copy.wait_recv()
    scale = columns[pl.ds(pl.multiple_of(me * cp, 8), cp), :][:, 2 * basis:2 * basis + 1]
    halo_two = halo(ext_two, 1)

    def normalise(i):
        j = rows + i
        mean = totals[i // per, i % per][None, :] * (1.0 / chans)
        meansq = totals[j // per, j % per][None, :] * (1.0 / chans)
        v = first[i].astype(F32)
        v = (v - mean) * lax.rsqrt(meansq - mean * mean + 1e-05) * scale
        ext_two[(HALO + i) * cp:(HALO + i + 1) * cp, :] = v.astype(BF16)

    edges = list(range(HALO)) + list(range(rows - HALO, rows))
    for i in edges:
        normalise(i)
    for copy in halo_two:
        copy.start()
    for i in range(HALO, rows - HALO):
        normalise(i)
    spectrum = mix(ext_two, halo_two, spec_two, basis)
    second_t[...] = lax.dot_general(
        inverse_t[...], spectrum, (((1,), (1,)), ((), ())), preferred_element_type=F32
    ).astype(BF16).reshape(second_t.shape)
    copies_d = exchange(lambda o: second_t.at[peer(o)], out.at[me], d_send, d_recv)
    for copy in copies_d:
        copy.start()
    for copy in copies_v:
        copy.wait_recv()
    for copy in copies_w:
        copy.start()
    out[me] = second_t[me]
    for copy in copies_d + copies_w:
        copy.wait_recv()
    for copy in copies_a + copies_b + copies_c + copies_d + copies_u + copies_v + copies_w:
        copy.wait_send()
    for copy in halo_one + halo_two:
        copy.wait_send()


def mlp_kernel(n, part, cp, blocks, field, w_in, w_out, result, cells):
    rows, lons, chans = field.shape
    lon_pad = blocks.shape[1]
    for i in range(rows):
        for s in range(n):
            piece = blocks[s, :, i * cp:i * cp + part]
            cells[i * lon_pad:(i + 1) * lon_pad, s * part:(s + 1) * part] = piece
    chunk = 4 if rows % 4 == 0 else 1

    for j in range(rows // chunk):
        x = cells[j * chunk * lon_pad:(j + 1) * chunk * lon_pad, :]
        hidden = lax.dot_general(
            x, w_in[...], (((1,), (1,)), ((), ())), preferred_element_type=F32)
        hidden = jax.nn.gelu(hidden).astype(BF16)
        update = jnp.dot(hidden, w_out[...], preferred_element_type=F32)
        update = update.reshape(chunk, lon_pad, chans)[:, :lons, :]
        for q in range(chunk):
            i = j * chunk + q
            result[i] = (field[i].astype(F32) + update[q]).astype(BF16)


def shards(n, n_lat, field, support, spec_one, theta_one, spec_two, theta_two, norm_gain, w_in, w_out):
    rows, chans, lons = field.shape
    circle = lons * n
    half = circle // 2
    part = chans // n
    cp = round_up(part, 16)
    lon_pad = round_up(lons, 16)
    mode_pad = round_up(half, 128)
    forward, inverse, inverse_t = tables(circle, n, lons, lon_pad, mode_pad)

    def spread(x, axis):
        if cp == part:
            return x
        shape = x.shape
        x = x.reshape(shape[:axis] + (n, part) + shape[axis + 1:])
        pads = [(0, 0)] * x.ndim
        pads[axis + 1] = (0, cp - part)
        return jnp.pad(x, pads).reshape(shape[:axis] + (n * cp,) + shape[axis + 1:])

    per = -(-2 * rows // n)
    lanes = n * lon_pad
    vmem = pl.BlockSpec(memory_space=pltpu.VMEM)
    smem = pl.BlockSpec(memory_space=pltpu.SMEM)
    pair = pltpu.SemaphoreType.DMA((n,))
    piece = w_in.shape[0] // n_lat
    gather = n % CORES == 0 and w_in.shape[0] % n_lat == 0 and piece % 16 == 0
    if not gather:
        piece = 16
    weights = jax.ShapeDtypeStruct((CORES, n_lat, n // CORES, piece, chans), BF16)
    out, piece_in, piece_out = pl.pallas_call(
        functools.partial(conv_kernel, n, n_lat, chans, half, gather),
        out_shape=(jax.ShapeDtypeStruct((n, lon_pad, rows * cp), BF16), weights, weights),
        in_specs=[smem] + [vmem] * 11,
        out_specs=(vmem, vmem, vmem),
        scratch_shapes=[
            pltpu.VMEM((n, lon_pad, rows * cp), BF16),
            pltpu.VMEM((lanes, rows * cp), BF16),
            pltpu.VMEM(((rows + 2 * HALO) * cp, lanes), BF16),
            pltpu.VMEM(((rows + 2 * HALO) * cp, lanes), BF16),
            pltpu.VMEM((rows + 2 * HALO, cp, 2 * mode_pad), F32),
            pltpu.VMEM((rows, cp, 2 * mode_pad), BF16),
            pltpu.VMEM((rows, cp, lanes), BF16),
            pltpu.VMEM((n, per, lanes), F32),
            pltpu.VMEM((n, per, lanes), F32),
            pltpu.VMEM((n, per, lanes), F32),
            pltpu.VMEM((n, lon_pad, rows * cp), BF16),
            pltpu.VMEM((n * cp, round_up(2 * theta_one.shape[1] + 1, 8)), F32),
        ] + [pair] * 8 + [pltpu.SemaphoreType.DMA((2, 2))] * 2
        + [pltpu.SemaphoreType.DMA((2, max(1, n // CORES)))] * 2
        + [pltpu.SemaphoreType.DMA((2, n_lat))] * 2
        + [pltpu.SemaphoreType.DMA((2,))] * 2,
        compiler_params=pltpu.CompilerParams(
            collective_id=0, has_side_effects=True, vmem_limit_bytes=50 * 2**20),
        name="convs",
    )(
        support.T, spread(field.transpose(0, 2, 1), 2), forward, inverse, inverse_t,
        spec_one.transpose(1, 2, 3, 0, 4), spread(theta_one.T, 1),
        spec_two.transpose(1, 2, 3, 0, 4), spread(theta_two.T, 1),
        spread(norm_gain[None, :], 1), w_in, w_out,
    )
    if gather:
        piece_in, piece_out = piece_in.reshape(-1, chans), piece_out.reshape(-1, chans)
    else:
        piece_in = lax.all_gather(w_in, "lon", axis=0, tiled=True)
        piece_out = lax.all_gather(w_out, "lon", axis=0, tiled=True)
    result = pl.pallas_call(
        functools.partial(mlp_kernel, n, part, cp),
        out_shape=jax.ShapeDtypeStruct((rows, lons, chans), BF16),
        in_specs=[vmem] * 4,
        out_specs=vmem,
        scratch_shapes=[pltpu.VMEM((rows * lon_pad, chans), BF16)],
        compiler_params=pltpu.CompilerParams(vmem_limit_bytes=40 * 2**20),
        name="mlp",
    )(out, field.transpose(0, 2, 1), piece_in, piece_out)
    return result.transpose(0, 2, 1)


def solution(mesh):
    in_specs = (
        P("lat", None, "lon"),
        P("lat", None),
        P(None, None, "lat", None, None),
        P(),
        P(None, None, "lat", None, None),
        P(),
        P(),
        P("lon", None),
        P("lon", None),
    )
    body = functools.partial(shards, mesh.shape["lon"], mesh.shape["lat"])
    return jax.shard_map(
        body, mesh=mesh, in_specs=in_specs, out_specs=P("lat", None, "lon"), check_vma=False)
```

```python
import functools
import math

import jax
import jax.numpy as jnp
import numpy as np
from jax import lax
from jax.experimental import pallas as pl
from jax.experimental.pallas import tpu as pltpu
from jax.sharding import PartitionSpec as P

HALO = 2
CORES = 2
MESH = pl.DeviceIdType.MESH
F32 = jnp.float32
BF16 = jnp.bfloat16


def round_up(value, step):
    return -(-value // step) * step


def tables(circle, n, lons, lon_pad, mode_pad):
    half = circle // 2
    grid = np.arange(circle)[:, None] * np.arange(half)[None, :] % circle
    phase = grid.astype(np.float64) * (2.0 * math.pi / circle)
    cos, sin = np.cos(phase), np.sin(phase)
    weights = np.where(np.arange(half) == 0, 1.0, 2.0) / circle
    forward = np.zeros((n, lon_pad, 2, mode_pad), np.float32)
    forward[:, :lons, 0, :half] = cos.reshape(n, lons, half)
    forward[:, :lons, 1, :half] = -sin.reshape(n, lons, half)
    inverse_t = np.zeros((n, lon_pad, 2, mode_pad), np.float32)
    inverse_t[:, :lons, 0, :half] = (cos * weights).reshape(n, lons, half)
    inverse_t[:, :lons, 1, :half] = (-sin * weights).reshape(n, lons, half)
    forward = forward.reshape(n * lon_pad, 2 * mode_pad)
    inverse_t = inverse_t.reshape(n * lon_pad, 2 * mode_pad)
    return [jnp.asarray(t, BF16) for t in (forward, inverse_t.T, inverse_t)]


def conv_kernel(
    n, n_lat, chans, half, gather, loads,
    support, field, forward, inverse, inverse_t, spec_one, theta_one, spec_two, theta_two, gain, w_in, w_out,
    out, all_in, all_out,
    send_t, circ_t, ext_one, ext_two, spectra, packed, first, part, sums, totals, second_t,
    columns,
    a_send, a_recv, b_send, b_recv, c_send, c_recv, d_send, d_recv, h_send, h_recv,
    u_send, u_recv, v_send, v_recv, w_send, w_recv,
):
    rows = field.shape[0]
    lons = field.shape[1]
    cp = field.shape[2] // n
    lon_pad = send_t.shape[1]
    mode_pad = forward.shape[1] // 2
    me = lax.axis_index("lon")
    lat = lax.axis_index("lat")
    up = lax.rem(lat + 1, n_lat)
    down = lax.rem(lat + n_lat - 1, n_lat)
    per = part.shape[1]

    def peer(o):
        return lax.rem(me + o, n)

    barrier = pltpu.get_barrier_semaphore()
    for o in range(1, n):
        pl.semaphore_signal(barrier, inc=1, device_id=(lat, peer(o)), device_id_type=MESH)
    for o in range(1, n_lat):
        pl.semaphore_signal(
            barrier, inc=1, device_id=(lax.rem(lat + o, n_lat), me), device_id_type=MESH)

    def exchange(srcs, dst, send, recv):
        copies = []
        for o in range(1, n):
            copies.append(pltpu.make_async_remote_copy(
                src_ref=srcs(o), dst_ref=dst, send_sem=send.at[o], recv_sem=recv.at[o],
                device_id=(lat, peer(o)), device_id_type=MESH))
        return copies

    mine = pl.multiple_of(me * lon_pad, 16)
    copies_a = exchange(lambda o: send_t.at[peer(o)], circ_t.at[pl.ds(mine, lon_pad)], a_send, a_recv)
    send_t[...] = jnp.zeros_like(send_t)
    loads[0].wait()
    for i in range(rows):
        x = field[i]
        for d in range(n):
            send_t[d, :lons, i * cp:(i + 1) * cp] = x[:, d * cp:(d + 1) * cp]
    pl.semaphore_wait(barrier, n + n_lat - 2)
    for copy in copies_a:
        copy.start()
    circ_t[pl.ds(mine, lon_pad)] = send_t[me]
    for load in loads[1:]:
        load.wait()
    basis = theta_one.shape[0]
    stack = [theta_one[...], theta_two[...], gain[...]]
    stack.append(jnp.zeros((round_up(2 * basis + 1, 8) - 2 * basis - 1, n * cp), F32))
    columns[...] = jnp.concatenate(stack, axis=0).T
    packed[...] = jnp.zeros_like(packed)
    part[...] = jnp.zeros_like(part)

    pairs = ((w_in, all_in), (w_out, all_out)) if gather else ()
    core = lax.rem(me, CORES)
    chip = me // CORES

    def remote(src, dst, send, recv, device):
        return pltpu.make_async_remote_copy(
            src_ref=src, dst_ref=dst, send_sem=send, recv_sem=recv,
            device_id=device, device_id_type=MESH)

    copies_u, copies_v, copies_w = [], [], []
    for m, (shard, whole) in enumerate(pairs):
        piece = whole.shape[3]
        share = pl.ds(pl.multiple_of(lat * piece, 16), piece)
        for o in range(1, n // CORES):
            copies_u.append(remote(
                shard.at[share], whole.at[core, lat, chip], u_send.at[m, o], u_recv.at[m, o],
                (lat, peer(CORES * o))))
        for o in range(1, n_lat):
            copies_v.append(remote(
                whole.at[core, lat], whole.at[core, lat], v_send.at[m, o], v_recv.at[m, o],
                (lax.rem(lat + o, n_lat), me)))
        copies_w.append(remote(
            whole.at[core], whole.at[core], w_send.at[m], w_recv.at[m],
            (lat, me + 1 - 2 * core)))
        whole[core, lat, chip] = shard[share, :]

    own = slice(HALO * cp, (HALO + rows) * cp)

    def halo(ext, which):
        width = HALO * cp
        low = pltpu.make_async_remote_copy(
            src_ref=ext.at[pl.ds(width, width)], dst_ref=ext.at[pl.ds(width + rows * cp, width)],
            send_sem=h_send.at[which, 0], recv_sem=h_recv.at[which, 0],
            device_id=(down, me), device_id_type=MESH)
        high = pltpu.make_async_remote_copy(
            src_ref=ext.at[pl.ds(rows * cp, width)], dst_ref=ext.at[pl.ds(0, width)],
            send_sem=h_send.at[which, 1], recv_sem=h_recv.at[which, 1],
            device_id=(up, me), device_id_type=MESH)
        return low, high

    def mix(ext, halos, spec, theta):
        def dft(start, count):
            x = ext[start * cp:(start + count) * cp, :]
            spectra[start:start + count] = jnp.dot(
                x, forward[...], preferred_element_type=F32).reshape(count, cp, 2 * mode_pad)

        dft(HALO, rows)
        th = columns[pl.ds(pl.multiple_of(me * cp, 8), cp), :]
        cols = [th[:, theta + b:theta + b + 1] for b in range(basis)]

        def row(i, carry):
            p_re = jnp.zeros((cp, half), F32)
            p_im = jnp.zeros((cp, half), F32)
            for k in range(support.shape[0]):
                r = jnp.clip(support[k, i] - lat * rows + HALO, 0, rows + 2 * HALO - 1)
                g = spectra[r]
                g_re, g_im = g[:, :half], g[:, mode_pad:mode_pad + half]
                w_re = sum(cols[b] * spec[b, i, k][0:1, :] for b in range(len(cols)))
                w_im = sum(cols[b] * spec[b, i, k][1:2, :] for b in range(len(cols)))
                p_re += w_re * g_re - w_im * g_im
                p_im += w_re * g_im + w_im * g_re
            packed[i, :, :half] = p_re.astype(BF16)
            packed[i, :, mode_pad:mode_pad + half] = p_im.astype(BF16)
            return carry

        inner = (HALO, rows - HALO) if rows > 2 * HALO else (0, 0)
        lax.fori_loop(inner[0], inner[1], row, 0)
        for copy in halos:
            copy.wait_recv()
        dft(0, HALO)
        dft(HALO + rows, HALO)
        if inner[1]:
            lax.fori_loop(0, HALO, row, 0)
            lax.fori_loop(rows - HALO, rows, row, 0)
        else:
            lax.fori_loop(0, rows, row, 0)
        return packed[...].reshape(rows * cp, 2 * mode_pad)

    for copy in copies_a:
        copy.wait_recv()
    ext_one[own, :] = circ_t[...].T
    halo_one = halo(ext_one, 0)
    for copy in halo_one:
        copy.start()
    for copy in copies_u:
        copy.start()
    spectrum = mix(ext_one, halo_one, spec_one, 0)
    values = jnp.dot(spectrum, inverse[...], preferred_element_type=F32).astype(BF16)
    first[...] = values.reshape(first.shape)

    for i in range(rows):
        v = first[i].astype(F32)
        part[i // per, i % per] = jnp.sum(v, axis=0)
        j = rows + i
        part[j // per, j % per] = jnp.sum(v * v, axis=0)
    copies_b = exchange(lambda o: part.at[peer(o)], sums.at[me], b_send, b_recv)
    for copy in copies_b:
        copy.start()
    sums[me] = part[me]
    for copy in copies_u:
        copy.wait_recv()
    for copy in copies_v:
        copy.start()
    for copy in copies_b:
        copy.wait_recv()
    totals[me] = jnp.sum(sums[...], axis=0)
    copies_c = exchange(lambda o: totals.at[me], totals.at[me], c_send, c_recv)
    for copy in copies_c:
        copy.start()
    for copy in copies_c:
        copy.wait_recv()
    scale = columns[pl.ds(pl.multiple_of(me * cp, 8), cp), :][:, 2 * basis:2 * basis + 1]
    halo_two = halo(ext_two, 1)

    def normalise(i):
        j = rows + i
        mean = totals[i // per, i % per][None, :] * (1.0 / chans)
        meansq = totals[j // per, j % per][None, :] * (1.0 / chans)
        v = first[i].astype(F32)
        v = (v - mean) * lax.rsqrt(meansq - mean * mean + 1e-05) * scale
        ext_two[(HALO + i) * cp:(HALO + i + 1) * cp, :] = v.astype(BF16)

    edges = list(range(HALO)) + list(range(rows - HALO, rows))
    for i in edges:
        normalise(i)
    for copy in halo_two:
        copy.start()
    for i in range(HALO, rows - HALO):
        normalise(i)
    spectrum = mix(ext_two, halo_two, spec_two, basis)
    second_t[...] = lax.dot_general(
        inverse_t[...], spectrum, (((1,), (1,)), ((), ())), preferred_element_type=F32
    ).astype(BF16).reshape(second_t.shape)
    copies_d = exchange(lambda o: second_t.at[peer(o)], out.at[me], d_send, d_recv)
    for copy in copies_d:
        copy.start()
    for copy in copies_v:
        copy.wait_recv()
    for copy in copies_w:
        copy.start()
    out[me] = second_t[me]
    for copy in copies_d + copies_w:
        copy.wait_recv()
    for copy in copies_a + copies_b + copies_c + copies_d + copies_u + copies_v + copies_w:
        copy.wait_send()
    for copy in halo_one + halo_two:
        copy.wait_send()


def conv_entry(n, n_lat, chans, half, gather, count, support, gain, *refs):
    held, rest = refs[:count], refs[count:-count - 1]
    local, sems = refs[-count - 1:-1], refs[-1]
    loads = [
        pltpu.make_async_copy(src, dst, sems.at[k]) for k, (src, dst) in enumerate(zip(held, local))
    ]
    for load in loads:
        load.start()
    conv_kernel(
        n, n_lat, chans, half, gather, loads, support, *local[:count - 2], gain, *local[count - 2:],
        *rest)


def mlp_kernel(
    n, part, cp, blocks_at, field_at, w_in_at, w_out_at,
    result, cells, blocks, field, w_in, w_out, sems,
):
    pairs = ((blocks_at, blocks), (w_in_at, w_in), (w_out_at, w_out), (field_at, field))
    loads = [pltpu.make_async_copy(src, dst, sems.at[k]) for k, (src, dst) in enumerate(pairs)]
    for load in loads:
        load.start()
    loads[0].wait()
    rows, lons, chans = field.shape
    lon_pad = blocks.shape[1]
    for i in range(rows):
        for s in range(n):
            piece = blocks[s, :, i * cp:i * cp + part]
            cells[i * lon_pad:(i + 1) * lon_pad, s * part:(s + 1) * part] = piece
    for load in loads[1:]:
        load.wait()
    chunk = 4 if rows % 4 == 0 else 1

    for j in range(rows // chunk):
        x = cells[j * chunk * lon_pad:(j + 1) * chunk * lon_pad, :]
        hidden = lax.dot_general(
            x, w_in[...], (((1,), (1,)), ((), ())), preferred_element_type=F32)
        hidden = jax.nn.gelu(hidden).astype(BF16)
        update = jnp.dot(hidden, w_out[...], preferred_element_type=F32)
        update = update.reshape(chunk, lon_pad, chans)[:, :lons, :]
        for q in range(chunk):
            i = j * chunk + q
            result[i] = (field[i].astype(F32) + update[q]).astype(BF16)


def shards(n, n_lat, field, support, spec_one, theta_one, spec_two, theta_two, norm_gain, w_in, w_out):
    rows, chans, lons = field.shape
    circle = lons * n
    half = circle // 2
    part = chans // n
    cp = round_up(part, 16)
    lon_pad = round_up(lons, 16)
    mode_pad = round_up(half, 128)
    forward, inverse, inverse_t = tables(circle, n, lons, lon_pad, mode_pad)

    def spread(x, axis):
        if cp == part:
            return x
        shape = x.shape
        x = x.reshape(shape[:axis] + (n, part) + shape[axis + 1:])
        pads = [(0, 0)] * x.ndim
        pads[axis + 1] = (0, cp - part)
        return jnp.pad(x, pads).reshape(shape[:axis] + (n * cp,) + shape[axis + 1:])

    per = -(-2 * rows // n)
    lanes = n * lon_pad
    vmem = pl.BlockSpec(memory_space=pltpu.VMEM)
    smem = pl.BlockSpec(memory_space=pltpu.SMEM)
    pair = pltpu.SemaphoreType.DMA((n,))
    piece = w_in.shape[0] // n_lat
    gather = n % CORES == 0 and w_in.shape[0] % n_lat == 0 and piece % 16 == 0
    if not gather:
        piece = 16
    weights = jax.ShapeDtypeStruct((CORES, n_lat, n // CORES, piece, chans), BF16)
    held = [
        spread(field.transpose(0, 2, 1), 2), forward, inverse, inverse_t,
        spec_one.transpose(1, 2, 3, 0, 4), spread(theta_one.T, 1),
        spec_two.transpose(1, 2, 3, 0, 4), spread(theta_two.T, 1), w_in, w_out,
    ]
    out, piece_in, piece_out = pl.pallas_call(
        functools.partial(conv_entry, n, n_lat, chans, half, gather, len(held)),
        out_shape=(jax.ShapeDtypeStruct((n, lon_pad, rows * cp), BF16), weights, weights),
        in_specs=[smem, vmem] + [pl.BlockSpec(memory_space=pl.ANY)] * len(held),
        out_specs=(vmem, vmem, vmem),
        scratch_shapes=[
            pltpu.VMEM((n, lon_pad, rows * cp), BF16),
            pltpu.VMEM((lanes, rows * cp), BF16),
            pltpu.VMEM(((rows + 2 * HALO) * cp, lanes), BF16),
            pltpu.VMEM(((rows + 2 * HALO) * cp, lanes), BF16),
            pltpu.VMEM((rows + 2 * HALO, cp, 2 * mode_pad), F32),
            pltpu.VMEM((rows, cp, 2 * mode_pad), BF16),
            pltpu.VMEM((rows, cp, lanes), BF16),
            pltpu.VMEM((n, per, lanes), F32),
            pltpu.VMEM((n, per, lanes), F32),
            pltpu.VMEM((n, per, lanes), F32),
            pltpu.VMEM((n, lon_pad, rows * cp), BF16),
            pltpu.VMEM((n * cp, round_up(2 * theta_one.shape[1] + 1, 8)), F32),
        ] + [pair] * 8 + [pltpu.SemaphoreType.DMA((2, 2))] * 2
        + [pltpu.SemaphoreType.DMA((2, max(1, n // CORES)))] * 2
        + [pltpu.SemaphoreType.DMA((2, n_lat))] * 2
        + [pltpu.SemaphoreType.DMA((2,))] * 2
        + [pltpu.VMEM(x.shape, x.dtype) for x in held] + [pltpu.SemaphoreType.DMA((len(held),))],
        compiler_params=pltpu.CompilerParams(
            collective_id=0, has_side_effects=True, vmem_limit_bytes=60 * 2**20),
        name="convs",
    )(
        support.T, spread(norm_gain[None, :], 1), *held,
    )
    if gather:
        piece_in, piece_out = piece_in.reshape(-1, chans), piece_out.reshape(-1, chans)
    else:
        piece_in = lax.all_gather(w_in, "lon", axis=0, tiled=True)
        piece_out = lax.all_gather(w_out, "lon", axis=0, tiled=True)
    result = pl.pallas_call(
        functools.partial(mlp_kernel, n, part, cp),
        out_shape=jax.ShapeDtypeStruct((rows, lons, chans), BF16),
        in_specs=[pl.BlockSpec(memory_space=pl.ANY)] * 4,
        out_specs=vmem,
        scratch_shapes=[
            pltpu.VMEM((rows * lon_pad, chans), BF16),
            pltpu.VMEM(out.shape, BF16),
            pltpu.VMEM((rows, lons, chans), BF16),
            pltpu.VMEM(piece_in.shape, BF16),
            pltpu.VMEM(piece_out.shape, BF16),
            pltpu.SemaphoreType.DMA((4,)),
        ],
        compiler_params=pltpu.CompilerParams(vmem_limit_bytes=60 * 2**20),
        name="mlp",
    )(out, field.transpose(0, 2, 1), piece_in, piece_out)
    return result.transpose(0, 2, 1)


def solution(mesh):
    in_specs = (
        P("lat", None, "lon"),
        P("lat", None),
        P(None, None, "lat", None, None),
        P(),
        P(None, None, "lat", None, None),
        P(),
        P(),
        P("lon", None),
        P("lon", None),
    )
    body = functools.partial(shards, mesh.shape["lon"], mesh.shape["lat"])
    return jax.shard_map(
        body, mesh=mesh, in_specs=in_specs, out_specs=P("lat", None, "lon"), check_vma=False)
```

```python
import functools
import math

import jax
import jax.numpy as jnp
import numpy as np
from jax import lax
from jax.experimental import pallas as pl
from jax.experimental.pallas import tpu as pltpu
from jax.sharding import PartitionSpec as P

HALO = 2
CORES = 2
MESH = pl.DeviceIdType.MESH
F32 = jnp.float32
BF16 = jnp.bfloat16


def round_up(value, step):
    return -(-value // step) * step


def tables(circle, n, lons, lon_pad, mode_pad):
    half = circle // 2
    grid = np.arange(circle)[:, None] * np.arange(half)[None, :] % circle
    phase = grid.astype(np.float64) * (2.0 * math.pi / circle)
    cos, sin = np.cos(phase), np.sin(phase)
    weights = np.where(np.arange(half) == 0, 1.0, 2.0) / circle
    forward = np.zeros((n, lon_pad, 2, mode_pad), np.float32)
    forward[:, :lons, 0, :half] = cos.reshape(n, lons, half)
    forward[:, :lons, 1, :half] = -sin.reshape(n, lons, half)
    inverse_t = np.zeros((n, lon_pad, 2, mode_pad), np.float32)
    inverse_t[:, :lons, 0, :half] = (cos * weights).reshape(n, lons, half)
    inverse_t[:, :lons, 1, :half] = (-sin * weights).reshape(n, lons, half)
    forward = forward.reshape(n * lon_pad, 2 * mode_pad)
    inverse_t = inverse_t.reshape(n * lon_pad, 2 * mode_pad)
    return [jnp.asarray(t, BF16) for t in (forward, inverse_t.T, inverse_t)]


def conv_kernel(
    n, n_lat, chans, half, gather, loads,
    support, field, forward, inverse, inverse_t, spec_one, theta_one, spec_two, theta_two, gain, w_in, w_out,
    out, all_in, all_out,
    send_t, circ_t, ext_one, ext_two, spectra, packed, first, part, sums, totals, second_t,
    columns,
    a_send, a_recv, b_send, b_recv, c_send, c_recv, d_send, d_recv, h_send, h_recv,
    u_send, u_recv, v_send, v_recv, w_send, w_recv,
):
    rows = field.shape[0]
    lons = field.shape[1]
    cp = field.shape[2] // n
    lon_pad = send_t.shape[1]
    mode_pad = forward.shape[1] // 2
    me = lax.axis_index("lon")
    lat = lax.axis_index("lat")
    up = lax.rem(lat + 1, n_lat)
    down = lax.rem(lat + n_lat - 1, n_lat)
    per = part.shape[1]

    def peer(o):
        return lax.rem(me + o, n)

    barrier = pltpu.get_barrier_semaphore()
    for o in range(1, n):
        pl.semaphore_signal(barrier, inc=1, device_id=(lat, peer(o)), device_id_type=MESH)
    for o in range(1, n_lat):
        pl.semaphore_signal(
            barrier, inc=1, device_id=(lax.rem(lat + o, n_lat), me), device_id_type=MESH)

    def exchange(srcs, dst, send, recv):
        copies = []
        for o in range(1, n):
            copies.append(pltpu.make_async_remote_copy(
                src_ref=srcs(o), dst_ref=dst, send_sem=send.at[o], recv_sem=recv.at[o],
                device_id=(lat, peer(o)), device_id_type=MESH))
        return copies

    mine = pl.multiple_of(me * lon_pad, 16)
    copies_a = exchange(lambda o: send_t.at[peer(o)], circ_t.at[pl.ds(mine, lon_pad)], a_send, a_recv)
    send_t[...] = jnp.zeros_like(send_t)
    loads[0].wait()
    for i in range(rows):
        x = field[i]
        for d in range(n):
            send_t[d, :lons, i * cp:(i + 1) * cp] = x[:, d * cp:(d + 1) * cp]
    pl.semaphore_wait(barrier, n + n_lat - 2)
    for copy in copies_a:
        copy.start()
    circ_t[pl.ds(mine, lon_pad)] = send_t[me]
    for load in loads[1:]:
        load.wait()
    basis = theta_one.shape[0]
    stack = [theta_one[...], theta_two[...], gain[...].reshape(1, n * cp)]
    stack.append(jnp.zeros((round_up(2 * basis + 1, 8) - 2 * basis - 1, n * cp), F32))
    columns[...] = jnp.concatenate(stack, axis=0).T
    packed[...] = jnp.zeros_like(packed)
    part[...] = jnp.zeros_like(part)

    pairs = ((w_in, all_in), (w_out, all_out)) if gather else ()
    core = lax.rem(me, CORES)
    chip = me // CORES

    def remote(src, dst, send, recv, device):
        return pltpu.make_async_remote_copy(
            src_ref=src, dst_ref=dst, send_sem=send, recv_sem=recv,
            device_id=device, device_id_type=MESH)

    copies_u, copies_v, copies_w = [], [], []
    for m, (shard, whole) in enumerate(pairs):
        piece = whole.shape[3]
        share = pl.ds(pl.multiple_of(lat * piece, 16), piece)
        for o in range(1, n // CORES):
            copies_u.append(remote(
                shard.at[share], whole.at[core, lat, chip], u_send.at[m, o], u_recv.at[m, o],
                (lat, peer(CORES * o))))
        for o in range(1, n_lat):
            copies_v.append(remote(
                whole.at[core, lat], whole.at[core, lat], v_send.at[m, o], v_recv.at[m, o],
                (lax.rem(lat + o, n_lat), me)))
        copies_w.append(remote(
            whole.at[core], whole.at[core], w_send.at[m], w_recv.at[m],
            (lat, me + 1 - 2 * core)))
        whole[core, lat, chip] = shard[share, :]

    own = slice(HALO * cp, (HALO + rows) * cp)

    def halo(ext, which):
        width = HALO * cp
        low = pltpu.make_async_remote_copy(
            src_ref=ext.at[pl.ds(width, width)], dst_ref=ext.at[pl.ds(width + rows * cp, width)],
            send_sem=h_send.at[which, 0], recv_sem=h_recv.at[which, 0],
            device_id=(down, me), device_id_type=MESH)
        high = pltpu.make_async_remote_copy(
            src_ref=ext.at[pl.ds(rows * cp, width)], dst_ref=ext.at[pl.ds(0, width)],
            send_sem=h_send.at[which, 1], recv_sem=h_recv.at[which, 1],
            device_id=(up, me), device_id_type=MESH)
        return low, high

    def mix(ext, halos, spec, theta):
        def dft(start, count):
            x = ext[start * cp:(start + count) * cp, :]
            spectra[start:start + count] = jnp.dot(
                x, forward[...], preferred_element_type=F32).reshape(count, cp, 2 * mode_pad)

        dft(HALO, rows)
        th = columns[pl.ds(pl.multiple_of(me * cp, 8), cp), :]
        cols = [th[:, theta + b:theta + b + 1] for b in range(basis)]

        def row(i, carry):
            p_re = jnp.zeros((cp, half), F32)
            p_im = jnp.zeros((cp, half), F32)
            for k in range(support.shape[0]):
                r = jnp.clip(support[k, i] - lat * rows + HALO, 0, rows + 2 * HALO - 1)
                g = spectra[r]
                g_re, g_im = g[:, :half], g[:, mode_pad:mode_pad + half]
                w_re = sum(cols[b] * spec[b, i, k][0:1, :] for b in range(len(cols)))
                w_im = sum(cols[b] * spec[b, i, k][1:2, :] for b in range(len(cols)))
                p_re += w_re * g_re - w_im * g_im
                p_im += w_re * g_im + w_im * g_re
            packed[i, :, :half] = p_re.astype(BF16)
            packed[i, :, mode_pad:mode_pad + half] = p_im.astype(BF16)
            return carry

        inner = (HALO, rows - HALO) if rows > 2 * HALO else (0, 0)
        lax.fori_loop(inner[0], inner[1], row, 0)
        for copy in halos:
            copy.wait_recv()
        dft(0, HALO)
        dft(HALO + rows, HALO)
        if inner[1]:
            lax.fori_loop(0, HALO, row, 0)
            lax.fori_loop(rows - HALO, rows, row, 0)
        else:
            lax.fori_loop(0, rows, row, 0)
        return packed[...].reshape(rows * cp, 2 * mode_pad)

    for copy in copies_a:
        copy.wait_recv()
    ext_one[own, :] = circ_t[...].T
    halo_one = halo(ext_one, 0)
    for copy in halo_one:
        copy.start()
    for copy in copies_u:
        copy.start()
    spectrum = mix(ext_one, halo_one, spec_one, 0)
    values = jnp.dot(spectrum, inverse[...], preferred_element_type=F32).astype(BF16)
    first[...] = values.reshape(first.shape)

    for i in range(rows):
        v = first[i].astype(F32)
        part[i // per, i % per] = jnp.sum(v, axis=0)
        j = rows + i
        part[j // per, j % per] = jnp.sum(v * v, axis=0)
    copies_b = exchange(lambda o: part.at[peer(o)], sums.at[me], b_send, b_recv)
    for copy in copies_b:
        copy.start()
    sums[me] = part[me]
    for copy in copies_u:
        copy.wait_recv()
    for copy in copies_v:
        copy.start()
    for copy in copies_b:
        copy.wait_recv()
    totals[me] = jnp.sum(sums[...], axis=0)
    copies_c = exchange(lambda o: totals.at[me], totals.at[me], c_send, c_recv)
    for copy in copies_c:
        copy.start()
    for copy in copies_c:
        copy.wait_recv()
    scale = columns[pl.ds(pl.multiple_of(me * cp, 8), cp), :][:, 2 * basis:2 * basis + 1]
    halo_two = halo(ext_two, 1)

    def normalise(i):
        j = rows + i
        mean = totals[i // per, i % per][None, :] * (1.0 / chans)
        meansq = totals[j // per, j % per][None, :] * (1.0 / chans)
        v = first[i].astype(F32)
        v = (v - mean) * lax.rsqrt(meansq - mean * mean + 1e-05) * scale
        ext_two[(HALO + i) * cp:(HALO + i + 1) * cp, :] = v.astype(BF16)

    edges = list(range(HALO)) + list(range(rows - HALO, rows))
    for i in edges:
        normalise(i)
    for copy in halo_two:
        copy.start()
    for i in range(HALO, rows - HALO):
        normalise(i)
    spectrum = mix(ext_two, halo_two, spec_two, basis)
    for copy in copies_v:
        copy.wait_recv()
    for copy in copies_w:
        copy.start()
    second_t[...] = lax.dot_general(
        inverse_t[...], spectrum, (((1,), (1,)), ((), ())), preferred_element_type=F32
    ).astype(BF16).reshape(second_t.shape)
    copies_d = exchange(lambda o: second_t.at[peer(o)], out.at[me], d_send, d_recv)
    for copy in copies_d:
        copy.start()
    out[me] = second_t[me]
    for copy in copies_d + copies_w:
        copy.wait_recv()
    for copy in copies_a + copies_b + copies_c + copies_d + copies_u + copies_v + copies_w:
        copy.wait_send()
    for copy in halo_one + halo_two:
        copy.wait_send()


def conv_entry(n, n_lat, chans, half, gather, count, support, gain, *refs):
    held, rest = refs[:count], refs[count:-count - 1]
    local, sems = refs[-count - 1:-1], refs[-1]
    loads = [
        pltpu.make_async_copy(src, dst, sems.at[k]) for k, (src, dst) in enumerate(zip(held, local))
    ]
    for load in loads:
        load.start()
    conv_kernel(
        n, n_lat, chans, half, gather, loads, support, *local[:count - 2], gain, *local[count - 2:],
        *rest)


def mlp_kernel(
    n, part, cp, blocks_at, field_at, w_in_at, w_out_at,
    result, cells, blocks, field, w_in, w_out, sems,
):
    pairs = ((blocks_at, blocks), (w_in_at, w_in), (w_out_at, w_out), (field_at, field))
    loads = [pltpu.make_async_copy(src, dst, sems.at[k]) for k, (src, dst) in enumerate(pairs)]
    for load in loads:
        load.start()
    loads[0].wait()
    rows, lons, chans = field.shape
    lon_pad = blocks.shape[1]
    for i in range(rows):
        for s in range(n):
            piece = blocks[s, :, i * cp:i * cp + part]
            cells[i * lon_pad:(i + 1) * lon_pad, s * part:(s + 1) * part] = piece
    for load in loads[1:]:
        load.wait()
    chunk = 4 if rows % 4 == 0 else 1

    for j in range(rows // chunk):
        x = cells[j * chunk * lon_pad:(j + 1) * chunk * lon_pad, :]
        hidden = lax.dot_general(
            x, w_in[...], (((1,), (1,)), ((), ())), preferred_element_type=F32)
        hidden = jax.nn.gelu(hidden).astype(BF16)
        update = jnp.dot(hidden, w_out[...], preferred_element_type=F32)
        update = update.reshape(chunk, lon_pad, chans)[:, :lons, :]
        for q in range(chunk):
            i = j * chunk + q
            result[i] = (field[i].astype(F32) + update[q]).astype(BF16)


def shards(n, n_lat, field, support, spec_one, theta_one, spec_two, theta_two, norm_gain, w_in, w_out):
    rows, chans, lons = field.shape
    circle = lons * n
    half = circle // 2
    part = chans // n
    cp = round_up(part, 16)
    lon_pad = round_up(lons, 16)
    mode_pad = round_up(half, 128)
    forward, inverse, inverse_t = tables(circle, n, lons, lon_pad, mode_pad)

    def spread(x, axis):
        if cp == part:
            return x
        shape = x.shape
        x = x.reshape(shape[:axis] + (n, part) + shape[axis + 1:])
        pads = [(0, 0)] * x.ndim
        pads[axis + 1] = (0, cp - part)
        return jnp.pad(x, pads).reshape(shape[:axis] + (n * cp,) + shape[axis + 1:])

    per = -(-2 * rows // n)
    lanes = n * lon_pad
    vmem = pl.BlockSpec(memory_space=pltpu.VMEM)
    smem = pl.BlockSpec(memory_space=pltpu.SMEM)
    pair = pltpu.SemaphoreType.DMA((n,))
    piece = w_in.shape[0] // n_lat
    gather = n % CORES == 0 and w_in.shape[0] % n_lat == 0 and piece % 16 == 0
    if not gather:
        piece = 16
    weights = jax.ShapeDtypeStruct((CORES, n_lat, n // CORES, piece, chans), BF16)
    held = [
        spread(field.transpose(0, 2, 1), 2), forward, inverse, inverse_t,
        spec_one.transpose(1, 2, 3, 0, 4), spread(theta_one.T, 1),
        spec_two.transpose(1, 2, 3, 0, 4), spread(theta_two.T, 1), w_in, w_out,
    ]
    out, piece_in, piece_out = pl.pallas_call(
        functools.partial(conv_entry, n, n_lat, chans, half, gather, len(held)),
        out_shape=(jax.ShapeDtypeStruct((n, lon_pad, rows * cp), BF16), weights, weights),
        in_specs=[smem, vmem] + [pl.BlockSpec(memory_space=pl.ANY)] * len(held),
        out_specs=(vmem, vmem, vmem),
        scratch_shapes=[
            pltpu.VMEM((n, lon_pad, rows * cp), BF16),
            pltpu.VMEM((lanes, rows * cp), BF16),
            pltpu.VMEM(((rows + 2 * HALO) * cp, lanes), BF16),
            pltpu.VMEM(((rows + 2 * HALO) * cp, lanes), BF16),
            pltpu.VMEM((rows + 2 * HALO, cp, 2 * mode_pad), F32),
            pltpu.VMEM((rows, cp, 2 * mode_pad), BF16),
            pltpu.VMEM((rows, cp, lanes), BF16),
            pltpu.VMEM((n, per, lanes), F32),
            pltpu.VMEM((n, per, lanes), F32),
            pltpu.VMEM((n, per, lanes), F32),
            pltpu.VMEM((n, lon_pad, rows * cp), BF16),
            pltpu.VMEM((n * cp, round_up(2 * theta_one.shape[1] + 1, 8)), F32),
        ] + [pair] * 8 + [pltpu.SemaphoreType.DMA((2, 2))] * 2
        + [pltpu.SemaphoreType.DMA((2, max(1, n // CORES)))] * 2
        + [pltpu.SemaphoreType.DMA((2, n_lat))] * 2
        + [pltpu.SemaphoreType.DMA((2,))] * 2
        + [pltpu.VMEM(x.shape, x.dtype) for x in held] + [pltpu.SemaphoreType.DMA((len(held),))],
        compiler_params=pltpu.CompilerParams(
            collective_id=0, has_side_effects=True, vmem_limit_bytes=60 * 2**20),
        name="convs",
    )(
        support.T, spread(norm_gain, 0), *held,
    )
    if gather:
        piece_in, piece_out = piece_in.reshape(-1, chans), piece_out.reshape(-1, chans)
    else:
        piece_in = lax.all_gather(w_in, "lon", axis=0, tiled=True)
        piece_out = lax.all_gather(w_out, "lon", axis=0, tiled=True)
    result = pl.pallas_call(
        functools.partial(mlp_kernel, n, part, cp),
        out_shape=jax.ShapeDtypeStruct((rows, lons, chans), BF16),
        in_specs=[pl.BlockSpec(memory_space=pl.ANY)] * 4,
        out_specs=vmem,
        scratch_shapes=[
            pltpu.VMEM((rows * lon_pad, chans), BF16),
            pltpu.VMEM(out.shape, BF16),
            pltpu.VMEM((rows, lons, chans), BF16),
            pltpu.VMEM(piece_in.shape, BF16),
            pltpu.VMEM(piece_out.shape, BF16),
            pltpu.SemaphoreType.DMA((4,)),
        ],
        compiler_params=pltpu.CompilerParams(vmem_limit_bytes=60 * 2**20),
        name="mlp",
    )(out, field.transpose(0, 2, 1), piece_in, piece_out)
    return result.transpose(0, 2, 1)


def solution(mesh):
    in_specs = (
        P("lat", None, "lon"),
        P("lat", None),
        P(None, None, "lat", None, None),
        P(),
        P(None, None, "lat", None, None),
        P(),
        P(),
        P("lon", None),
        P("lon", None),
    )
    body = functools.partial(shards, mesh.shape["lon"], mesh.shape["lat"])
    return jax.shard_map(
        body, mesh=mesh, in_specs=in_specs, out_specs=P("lat", None, "lon"), check_vma=False)
```
